256 devices in a mesh: vocab: 64 (over z, y, core), tok: 4 (over x).
Axes of the slice: x: 4, y: 4, z: 8, core: 2. Of those that a mesh axis runs over, the one named last changes fastest.
Arguments:
- hidden: bfloat16 [1024, 3584], P('vocab', 'tok'), may hold values from -18 to 18
- head: bfloat16 [3584, 131072], P('tok', 'vocab'), may hold values from -0.15033445 to 0.15033445
- teacher: bfloat16 [1024, 131072], P(('tok', 'vocab')), may hold values from -18 to 320
- token_weight: float32 [1024], P('tok'), may hold values from 64 to 512
Outputs:
- grad_hidden: bfloat16 [1024, 3584], P('vocab', 'tok')
- grad_head: bfloat16 [3584, 131072], P('tok', 'vocab')
The draws below stay inside these ranges and needn't reach their ends.
All inputs are finite; a program needn't handle non-finite values.
Results may differ from the reference program's by a relative error of at most 0.0065.
Values may be sent and summed in bfloat16 or wider, within the bound.
A program may use at most 64 MiB of HBM per device.

```python
import math
import jax
import jax.numpy as jnp
from jax import lax

D = 3584
TOKENS = 1024
VOCAB = 131072


def column_block(key, index):
    return jnp.clip(jax.random.normal(jax.random.fold_in(key, index), (D, 128), jnp.float32), -8.0, 8.0)


def column_ramp(columns):
    return 0.9 + 0.2 * columns.astype(jnp.float32) / VOCAB


def head_values(key):
    blocks = jax.vmap(lambda number: column_block(key, number))(jnp.arange(VOCAB // 128, dtype=jnp.int32))
    return jnp.transpose(blocks, (1, 0, 2)).reshape(D, VOCAB)


def draw_head(key, part):
    base = head_values(key)
    sigma = D ** (-0.5) * column_ramp(jnp.arange(VOCAB, dtype=jnp.int32))[None, :]
    return (base * sigma).astype(jnp.bfloat16)


def draw_hidden(key, part):
    key = jax.random.fold_in(key, 23)
    return jnp.clip(jax.random.normal(key, (TOKENS, D), jnp.float32) * 3.0, -18.0, 18.0).astype(jnp.bfloat16)


def draw_teacher(key, part):
    key = jax.random.fold_in(key, 37)
    ramp = column_ramp(jnp.arange(VOCAB, dtype=jnp.int32))[None, :]
    return jnp.clip(jax.random.normal(key, (TOKENS, VOCAB), jnp.float32) * 3.0 * ramp, -18.0, 18.0).astype(jnp.bfloat16)


def shard_levels(stream_key, shape, cuts, smallest, top_value):
    def one(position, shards_of):
        steps = jax.random.uniform(jax.random.fold_in(jax.random.fold_in(stream_key, 6), position), (shards_of,), jnp.float32, smallest / len(cuts), top_value / len(cuts))
        return jnp.repeat(jnp.exp(steps), shape[position] // shards_of).reshape((-1,) + (1,) * (len(shape) - position - 1))

    gain = one(*cuts[0])
    for cut in cuts[1:]:
        gain = gain * one(*cut)
    return gain


def setup_inputs(seed: int = 0) -> dict:
    arg_keys = jax.random.split(jax.random.key(seed), 5)
    return {
        "hidden": draw_hidden(jax.random.fold_in(arg_keys[4], 71), 0),
        "head": draw_head(jax.random.fold_in(arg_keys[4], 71), 0),
        "teacher": draw_teacher(jax.random.fold_in(arg_keys[4], 71), 0),
        "token_weight": jnp.clip(jnp.exp(math.log(512.0) - 2.0794415 * jax.random.uniform(arg_keys[3], (TOKENS,), jnp.float32) ** shard_levels(arg_keys[3], (TOKENS,), ((0, 4),), -0.2, 0.2)), 64.0, 512.0),
    }


def reference(hidden, head, teacher, token_weight):
    block = 128
    count = TOKENS // block

    def one_block(index):
        start = (index * block).astype(jnp.int32)
        rows = lax.dynamic_slice_in_dim(hidden, start, block, 0)
        target_logits = lax.dynamic_slice_in_dim(teacher, start, block, 0).astype(jnp.float32)
        weight = lax.dynamic_slice_in_dim(token_weight, start, block, 0)
        logits = jnp.dot(rows, head, preferred_element_type=jnp.float32)
        student_exp = jnp.exp(logits - jnp.max(logits, axis=1, keepdims=True))
        student = student_exp / jnp.sum(student_exp, axis=1, keepdims=True)
        target_exp = jnp.exp(target_logits - jnp.max(target_logits, axis=1, keepdims=True))
        target = target_exp / jnp.sum(target_exp, axis=1, keepdims=True)
        return (weight[:, None] * (student - target)).astype(jnp.bfloat16)

    grads = lax.map(one_block, jnp.arange(count, dtype=jnp.int32))
    grad_logits = grads.reshape(TOKENS, VOCAB)
    grad_hidden = jnp.dot(grad_logits, head.T, preferred_element_type=jnp.float32).astype(jnp.bfloat16)
    grad_head = jnp.dot(hidden.T, grad_logits, preferred_element_type=jnp.float32).astype(jnp.bfloat16)
    return grad_hidden, grad_head
```

```python
import jax
import jax.numpy as jnp
from jax import lax
from jax.experimental import pallas as pl
from jax.experimental.pallas import tpu as pltpu
from jax.sharding import PartitionSpec as P

MESH = pl.DeviceIdType.MESH
F32, BF16 = jnp.float32, jnp.bfloat16
NX, NZ, NY, NC = 4, 8, 4, 2
YC = NY * NC
RB = 16
POWER = 9


class Copies:
    def __init__(self, send, recv):
        self.send, self.recv, self.count, self.started = send, recv, 0, []

    def make(self, src, dst, vocab, tok):
        n = self.count
        self.count += 1
        return pltpu.make_async_remote_copy(
            src_ref=src,
            dst_ref=dst,
            send_sem=self.send.at[n],
            recv_sem=self.recv.at[n],
            device_id={"vocab": vocab, "tok": tok},
            device_id_type=MESH,
        )

    def start(self, src, dst, vocab, tok):
        copy = self.make(src, dst, vocab, tok)
        copy.start()
        self.started.append(copy)
        return copy


def encode(p):
    p2 = p * p
    p4 = p2 * p2
    return (p4 * p4 * p).astype(BF16)


def decode(x):
    x = x.astype(F32)
    root = jnp.exp(jnp.log(jnp.abs(x)) * (1.0 / POWER))
    return jnp.where(x < 0.0, -root, root)


def eye():
    return lax.broadcasted_iota(jnp.int32, (128, 128), 0) == lax.broadcasted_iota(jnp.int32, (128, 128), 1)


def to_row(wide):
    return jnp.sum(jnp.where(eye(), wide, 0.0), axis=0, keepdims=True)


def to_column(row):
    return jnp.sum(jnp.where(eye(), jnp.broadcast_to(row, (128, 128)), 0.0), axis=1, keepdims=True)


def tile(*rows):
    return jnp.concatenate(list(rows) + [jnp.zeros((8 - len(rows), 128), F32)], axis=0)


def merge(ref, h):
    peak = ref[h, 0, 0:1, :]
    tpeak = ref[h, 0, 2:3, :]
    for i in range(1, 8):
        peak = jnp.maximum(peak, ref[h, i, 0:1, :])
        tpeak = jnp.maximum(tpeak, ref[h, i, 2:3, :])
    total = jnp.zeros_like(peak)
    ttotal = jnp.zeros_like(peak)
    for i in range(8):
        total += ref[h, i, 1:2, :] * jnp.exp(ref[h, i, 0:1, :] - peak)
        ttotal += ref[h, i, 3:4, :] * jnp.exp(ref[h, i, 2:3, :] - tpeak)
    return peak, total, tpeak, ttotal


def kernel(
    hidden, head, teacher, weight, gh_out, gw_out,
    hid, headv, tmid, tfin, te, po, to_l, to_r, r_opp, from_l, from_r, own, acc_l, acc_r,
    stc, st0, st1, st1m, st2, fac, gbuf, acc, at, gwb,
    ghp, ghr, zs, zr, gho, local, send, recv, zsend, zrecv,
):
    v, me = lax.axis_index("vocab"), lax.axis_index("tok")
    z, yc = v // YC, v % YC
    y, c = yc // NC, yc % NC
    left, right, opp = (me + NX - 1) % NX, (me + 1) % NX, (me + 2) % NX
    blocks = (opp, right, left, me)
    width, cols = headv.shape
    chunk = min(512, cols)
    chunks = cols // chunk
    cp = Copies(send, recv)

    def zpeer(k):
        return ((z + k) % NZ) * YC + yc

    def ycpeer(k):
        return z * YC + (yc + k) % YC

    get_head = pltpu.make_async_copy(head, headv, local.at[0])
    get_head.start()
    get_hidden = pltpu.make_async_copy(hidden, hid.at[z, y, c], local.at[1])
    get_hidden.start()
    get_teacher = pltpu.make_async_copy(teacher.at[:, yc], tmid.at[yc], local.at[2])
    get_teacher.start()

    barrier = pltpu.get_barrier_semaphore()
    for k in range(1, NZ):
        pl.semaphore_signal(barrier, inc=1, device_id={"vocab": zpeer(k), "tok": me}, device_id_type=MESH)
    for k in range(1, YC):
        pl.semaphore_signal(barrier, inc=1, device_id={"vocab": ycpeer(k), "tok": me}, device_id_type=MESH)
    for x in (left, right):
        pl.semaphore_signal(barrier, inc=1, device_id={"vocab": v, "tok": x}, device_id_type=MESH)
    pl.semaphore_wait(barrier, NZ - 1 + YC - 1 + 2)

    hz = [cp.start(hidden, hid.at[z, y, c], zpeer(k), me) for k in range(1, NZ)]
    tyc = [cp.start(teacher.at[:, (yc + k) % YC], tmid.at[yc], ycpeer(k), me) for k in range(1, YC)]
    get_hidden.wait()
    for copy in hz:
        copy.wait_recv()
    hy = []
    for d in blocks:
        part = hid.at[pl.ds(2 * d, 2), y, c]
        hy.append([cp.start(part, part, ycpeer(NC * k), me) for k in range(1, NY)])

    def rows_of(j):
        for copy in hy[j]:
            copy.wait_recv()
        part = hid.at[pl.ds(2 * blocks[j], 2), :, c]
        return cp.start(part, part, ycpeer_sibling, me)

    ycpeer_sibling = z * YC + y * NC + (1 - c)

    def hidden_rows(d):
        return hid[pl.ds(2 * d, 2)].reshape(2 * YC * RB, width)

    def partial(j, write):
        def step(q, _):
            here = pl.ds(pl.multiple_of(q * chunk, chunk), chunk)
            p = jnp.dot(hidden_rows(blocks[j]), headv[:, here], preferred_element_type=F32)
            write(here, p)
            return 0

        lax.fori_loop(0, chunks, step, 0)

    def write_opp(here, p):
        po[:, :, :, here] = encode(p.reshape(2, 2, 64, chunk))

    def write_right(here, p):
        p = p.reshape(2, 2, 64, chunk)
        to_r[:, 0, :, here] = encode(p[:, 0])
        acc_r[:, :, here] = p[:, 1]

    def write_left(here, p):
        p = p.reshape(2, 2, 64, chunk)
        to_l[:, 1, :, here] = encode(p[:, 1])
        acc_l[:, :, here] = p[:, 0]

    def write_own(here, p):
        own[:, :, here] = p.reshape(2, 128, chunk)

    sib = rows_of(0)
    sib.wait_recv()
    get_head.wait()
    partial(0, write_opp)

    def send_opp(h):
        return (
            cp.start(po.at[h, 0], r_opp.at[h, 0], v, left),
            cp.start(po.at[h, 1], r_opp.at[h, 1], v, right),
        )

    opp0 = send_opp(0)
    get_teacher.wait()
    for copy in tyc:
        copy.wait_recv()
    keep_teacher = pltpu.make_async_copy(tmid.at[:, z], tfin.at[pl.ds(z * YC, YC)], local.at[3])
    keep_teacher.start()
    tz = [
        cp.start(tmid.at[:, (z + k) % NZ], tfin.at[pl.ds(z * YC, YC)], zpeer(k), me)
        for k in range(1, NZ)
    ]
    sib = rows_of(1)
    sib.wait_recv()
    partial(1, write_right)
    right0 = cp.start(to_r.at[0, 0], from_l.at[0, 0], v, right)
    sib = rows_of(2)
    sib.wait_recv()
    partial(2, write_left)
    left0 = cp.start(to_l.at[0, 1], from_r.at[0, 1], v, left)
    opp1 = send_opp(1)
    sib = rows_of(3)

    def add_opp(h):
        def step(g, _):
            here = pl.ds(pl.multiple_of(g * 16, 16), 16)
            to_l[h, 0, here] = encode(acc_l[h, here] + decode(r_opp[h, 0, here]))
            to_r[h, 1, here] = encode(acc_r[h, here] + decode(r_opp[h, 1, here]))
            return 0

        lax.fori_loop(0, 4, step, 0)

    def send_sum(h):
        return (
            cp.start(to_l.at[h, 0], from_r.at[h, 0], v, left),
            cp.start(to_r.at[h, 1], from_l.at[h, 1], v, right),
        )

    for copy in opp0:
        copy.wait_recv()
    add_opp(0)
    sum0 = send_sum(0)
    right1 = cp.start(to_r.at[1, 0], from_l.at[1, 0], v, right)
    left1 = cp.start(to_l.at[1, 1], from_r.at[1, 1], v, left)
    sib.wait_recv()
    partial(3, write_own)
    for copy in opp1:
        copy.wait_recv()
    add_opp(1)
    sum1 = send_sum(1)

    keep_teacher.wait()
    for copy in tz:
        copy.wait_recv()

    def teacher_pair(p, _):
        h, q = p // 16, p % 16
        low = lax.broadcasted_iota(jnp.int32, (8, 8, 128), 1) < 4
        a = tfin[2 * p].astype(F32).reshape(8, 8, 128)
        b = tfin[2 * p + 1].astype(F32).reshape(8, 8, 128)
        even = jnp.where(low, a, pltpu.roll(b, 4, 1))
        odd = jnp.where(low, pltpu.roll(a, 4, 1), b)
        peak = jnp.max(jnp.max(jnp.maximum(even, odd), axis=0), axis=1, keepdims=True)
        even, odd = jnp.exp(even - peak), jnp.exp(odd - peak)
        total = jnp.sum(jnp.sum(even + odd, axis=0), axis=1, keepdims=True)
        here = pl.ds(pl.multiple_of(q * 8, 8), 8)
        for k in range(8):
            te[h, here, 256 * k : 256 * k + 128] = even[k]
            te[h, here, 256 * k + 128 : 256 * k + 256] = odd[k]
        stc[h, 2, here] = jnp.broadcast_to(peak, (8, 128))
        stc[h, 3, here] = jnp.broadcast_to(total, (8, 128))
        return 0

    lax.fori_loop(0, 32, teacher_pair, 0)

    def gradient(h, arrivals):
        for copy in arrivals:
            copy.wait_recv()

        def student(g, _):
            here = pl.ds(pl.multiple_of(g * 16, 16), 16)
            inside = pl.ds(pl.multiple_of((g % 4) * 16, 16), 16)
            half = g // 4
            logits = own[h, here] + decode(from_l[h, half, inside]) + decode(from_r[h, half, inside])
            peak = jnp.max(logits, axis=1, keepdims=True)
            exps = jnp.exp(logits - peak)
            own[h, here] = exps
            stc[h, 0, here] = jnp.broadcast_to(peak, (16, 128))
            stc[h, 1, here] = jnp.broadcast_to(jnp.sum(exps, axis=1, keepdims=True), (16, 128))
            return 0

        lax.fori_loop(0, 8, student, 0)
        mine = tile(to_row(stc[h, 0]), to_row(stc[h, 1]), to_row(stc[h, 2]), to_row(stc[h, 3]))
        st0[h] = mine
        st1[h, z] = mine
        over_z = [cp.start(st0.at[h], st1.at[h, z], zpeer(k), me) for k in range(1, NZ)]
        for copy in over_z:
            copy.wait_recv()
        plane = tile(*merge(st1, h))
        st1m[h] = plane
        st2[h, yc] = plane
        over_yc = [cp.start(st1m.at[h], st2.at[h, yc], ycpeer(k), me) for k in range(1, YC)]
        for copy in over_yc:
            copy.wait_recv()
        peak, total, tpeak, ttotal = merge(st2, h)
        w = weight[h : h + 1, :]
        fac[0] = jnp.broadcast_to(to_column(w * jnp.exp(st0[h, 0:1, :] - peak) / total), (128, 128))
        fac[1] = jnp.broadcast_to(to_column(w * jnp.exp(st0[h, 2:3, :] - tpeak) / ttotal), (128, 128))

        def write(g, _):
            here = pl.ds(pl.multiple_of(g * 16, 16), 16)
            gbuf[me, h, here] = (fac[0, here, :1] * own[h, here] - fac[1, here, :1] * te[h, here]).astype(BF16)
            return 0

        lax.fori_loop(0, 8, write, 0)
        return (
            cp.start(gbuf.at[me, h], gbuf.at[me, h], v, left),
            cp.start(gbuf.at[me, h], gbuf.at[me, h], v, right),
        )

    all0 = gradient(0, (right0, left0) + sum0)
    all1 = gradient(1, (right1, left1) + sum1)

    def hidden_partial(j, d):
        g = gbuf[d].reshape(256, cols)
        for n in range(0, width, 256):
            m = min(256, width - n)
            part = lax.dot_general(
                g, headv[n : n + m, :], (((1,), (1,)), ((), ())), preferred_element_type=F32
            )
            ghp[j, :, :, :, n : n + m] = part.reshape(2, YC, RB, m).astype(BF16)
        return [cp.start(ghp.at[j, :, (yc + k) % YC], ghr.at[j, k], ycpeer(k), me) for k in range(1, YC)]

    def hidden_sum(j, d, copies):
        for copy in copies:
            copy.wait_recv()
        total = ghp[j, :, yc].astype(F32)
        for k in range(1, YC):
            total += ghr[j, k].astype(F32)
        zs[j] = total
        for h in range(2):
            goal = 2 * d + h
            k = (goal - z + NZ) % NZ

            @pl.when(k != 0)
            def _():
                z_copy(j, h, goal, k).start()

            @pl.when(k == 0)
            def _():
                zr[0] = zs[j, h]

    def z_copy(j, h, goal, k):
        return pltpu.make_async_remote_copy(
            src_ref=zs.at[j, h],
            dst_ref=zr.at[k],
            send_sem=zsend.at[2 * j + h],
            recv_sem=zrecv.at[k],
            device_id={"vocab": goal * YC + yc, "tok": me},
            device_id_type=MESH,
        )

    def head_update(d, first, last):
        at[...] = hidden_rows(d).T

        def step(q, _):
            here = pl.ds(pl.multiple_of(q * chunk, chunk), chunk)
            part = jnp.dot(at[...], gbuf[d, :, :, here].reshape(256, chunk), preferred_element_type=F32)
            if not first:
                part = part + acc[:, here]
            if last:
                gwb[:, here] = part.astype(BF16)
                pltpu.make_async_copy(gwb.at[:, here], gw_out.at[:, here], local.at[4 + q]).start()
            else:
                acc[:, here] = part
            return 0

        lax.fori_loop(0, chunks, step, 0)

    def forward(h):
        all1_or_0 = all0 if h == 0 else all1
        all1_or_0[0].wait_recv()
        a = cp.start(gbuf.at[right, h, pl.ds(0, 64)], gbuf.at[right, h, pl.ds(0, 64)], v, left)
        all1_or_0[1].wait_recv()
        b = cp.start(gbuf.at[left, h, pl.ds(64, 64)], gbuf.at[left, h, pl.ds(64, 64)], v, right)
        return a, b

    gh_me = hidden_partial(0, me)
    fwd0 = forward(0)
    head_update(me, True, False)
    fwd1 = forward(1)
    gh_right = hidden_partial(1, right)
    gh_left = hidden_partial(2, left)
    hidden_sum(0, me, gh_me)
    head_update(right, False, False)
    hidden_sum(1, right, gh_right)
    head_update(left, False, False)
    hidden_sum(2, left, gh_left)
    for copy in fwd0 + fwd1:
        copy.wait_recv()
    gh_opp = hidden_partial(3, opp)
    head_update(opp, False, True)
    hidden_sum(3, opp, gh_opp)
    for k in range(1, NZ):
        z_copy(0, 0, z, k).wait_recv()
    total = zr[0]
    for k in range(1, NZ):
        total = total + zr[k]
    gho[...] = total.astype(BF16)
    put = pltpu.make_async_copy(gho, gh_out, local.at[1])
    put.start()

    for copy in cp.started:
        copy.wait_send()
    for j, d in enumerate((me, right, left, opp)):
        for h in range(2):
            goal = 2 * d + h
            k = (goal - z + NZ) % NZ

            @pl.when(k != 0)
            def _():
                z_copy(j, h, goal, k).wait_send()

    for q in range(chunks):
        here = pl.ds(q * chunk, chunk)
        pltpu.make_async_copy(gwb.at[:, here], gw_out.at[:, here], local.at[4 + q]).wait()
    put.wait()


def body(hidden, head, teacher, token_weight):
    width, cols = head.shape
    lanes = cols // 128
    blocks = teacher.reshape(4, NZ * YC, lanes, 128).transpose(1, 2, 0, 3).reshape(NZ, YC, 4 * lanes, 128)
    hbm = pl.BlockSpec(memory_space=pl.ANY)
    half = pltpu.VMEM((2, 2, 64, cols), BF16)
    return pl.pallas_call(
        kernel,
        out_shape=(
            jax.ShapeDtypeStruct((RB, width), BF16),
            jax.ShapeDtypeStruct((width, cols), BF16),
        ),
        in_specs=[hbm, hbm, hbm, pl.BlockSpec(memory_space=pltpu.VMEM)],
        out_specs=(hbm, hbm),
        scratch_shapes=[
            pltpu.VMEM((NZ, NY, NC, RB, width), BF16),
            pltpu.VMEM((width, cols), BF16),
            pltpu.VMEM((YC, NZ, 4 * lanes, 128), BF16),
            pltpu.VMEM((NZ * YC, 4 * lanes, 128), BF16),
            pltpu.VMEM((2, 128, cols), F32),
            half, half, half, half, half, half,
            pltpu.VMEM((2, 128, cols), F32),
            pltpu.VMEM((2, 64, cols), F32),
            pltpu.VMEM((2, 64, cols), F32),
            pltpu.VMEM((2, 4, 128, 128), F32),
            pltpu.VMEM((2, 8, 128), F32),
            pltpu.VMEM((2, NZ, 8, 128), F32),
            pltpu.VMEM((2, 8, 128), F32),
            pltpu.VMEM((2, YC, 8, 128), F32),
            pltpu.VMEM((2, 128, 128), F32),
            pltpu.VMEM((NX, 2, 128, cols), BF16),
            pltpu.VMEM((width, cols), F32),
            pltpu.VMEM((width, 256), BF16),
            pltpu.VMEM((width, cols), BF16),
            pltpu.VMEM((4, 2, YC, RB, width), BF16),
            pltpu.VMEM((4, YC, 2, RB, width), BF16),
            pltpu.VMEM((4, 2, RB, width), F32),
            pltpu.VMEM((NZ, RB, width), F32),
            pltpu.VMEM((RB, width), BF16),
            pltpu.SemaphoreType.DMA((8,)),
            pltpu.SemaphoreType.DMA((128,)),
            pltpu.SemaphoreType.DMA((128,)),
            pltpu.SemaphoreType.DMA((8,)),
            pltpu.SemaphoreType.DMA((8,)),
        ],
        compiler_params=pltpu.CompilerParams(
            collective_id=0, has_side_effects=True, vmem_limit_bytes=56 * 1024 * 1024
        ),
        cost_estimate=pl.CostEstimate(flops=11_274_289_152, bytes_accessed=9_000_000, transcendentals=1_048_576),
    )(hidden, head, blocks, token_weight.reshape(2, 128))


def solution(mesh):
    return jax.shard_map(
        body,
        mesh=mesh,
        in_specs=(P("vocab", "tok"), P("tok", "vocab"), P(("tok", "vocab"), None), P("tok")),
        out_specs=(P("vocab", "tok"), P("tok", "vocab")),
        check_vma=False,
    )
```
